128 devices in a mesh: loader: 16 (over z, x), shard: 8 (over y, core).
Axes of the slice: x: 4, y: 4, z: 4, core: 2. Of those that a mesh axis runs over, the one named last changes fastest.
Arguments:
- hidden_states: bfloat16 [262144, 768], P(('loader', 'shard')), may hold values from -6 to 6
- w_in: bfloat16 [768, 3072], replicated, may hold values from -0.21875 to 0.21875
- w_out: bfloat16 [3072, 768], replicated, may hold values from -0.109375 to 0.109375
- ln_gain: float32 [768], replicated, may hold values from 0.1 to 1.9
- passage_rows: int32 [1024], P(('loader', 'shard')), may hold values from 0 to 32767, as said below
- old_index: bfloat16 [32768, 768], P('shard'), may hold values from -1.2 to 1.2
- queries: bfloat16 [4096, 768], P('loader'), may hold values from -256 to 256
- candidates: int32 [4096, 64], P('loader'), may hold values from 0 to 32767, as said below
- teacher: float32 [4096, 64], P('loader'), may hold values from -8 to 304
Outputs:
- new_index: bfloat16 [32768, 768], P('shard')
- distill_loss: float32 [4096], P(('loader', 'shard'))
- query_grad: float32 [4096, 768], P(('loader', 'shard'))
The draws below stay inside these ranges and needn't reach their ends.
Inputs may be any that keep to these rules, and one draw needn't show every extreme that they name: `passage_rows`: distinct rows of the index; row r belongs to shard r // 4096. The 8 passages of one device name at most 2 rows of any one shard, and exactly 2 of some shard. `candidates`: rows of the index; a query may name a row twice.
All inputs are finite; a program needn't handle non-finite values.
Results may differ from the reference program's by a relative error of at most 0.0075.
Values may be sent and summed in bfloat16 or wider, within the bound.
A program may use at most 192 MiB of HBM per device.

```python
import math
import jax
import jax.numpy as jnp
from jax import lax

D = 768
FF = 3072
LEN = 256
K = 64
P_DEV = 8
R_SHARD = 4096
PASSAGES = 1024
INDEX_ROWS = 32768
QUERIES = 4096


def fresh_targets(key):
    key = jax.random.fold_in(key, 11)
    block_count = PASSAGES // P_DEV
    shard_count = INDEX_ROWS // R_SHARD
    bound = P_DEV // 4
    key_list = jax.random.split(key, 5)
    first_draw = jax.random.randint(key_list[0], (block_count,), 0, shard_count)
    second = jax.random.randint(key_list[1], (block_count,), 0, shard_count)
    hot_shard = first_draw * second // shard_count
    turn_draw = jax.random.randint(key_list[2], (block_count,), 0, shard_count - 1)
    slot_place = jnp.arange(P_DEV, dtype=jnp.int32)
    others = (hot_shard[:, None] + 1 + (slot_place[None, :] + turn_draw[:, None]) % (shard_count - 1)) % shard_count
    owner_shard = jnp.where(slot_place[None, :] < bound, hot_shard[:, None], others)
    shuffle_keys = jax.random.split(key_list[3], block_count)
    owner_shard = jax.vmap(lambda one_key, row_owners: jax.random.permutation(one_key, row_owners))(shuffle_keys, owner_shard)
    offsets = jax.random.permutation(key_list[4], R_SHARD)[:PASSAGES]
    return (owner_shard.reshape(-1) * R_SHARD + offsets).astype(jnp.int32)


def candidate_table(key):
    fresh_ids = fresh_targets(key)
    key = jax.random.fold_in(key, 13)
    shard_count = INDEX_ROWS // R_SHARD
    key_list = jax.random.split(key, 6)
    picked = jax.random.randint(key_list[0], (QUERIES, K), 0, PASSAGES)
    first_draw = jax.random.randint(key_list[1], (QUERIES, K), 0, shard_count)
    second = jax.random.randint(key_list[2], (QUERIES, K), 0, shard_count)
    owner_shard = first_draw * second // shard_count
    old_rows = owner_shard * R_SHARD + jax.random.randint(key_list[3], (QUERIES, K), 0, R_SHARD)
    use_fresh = jax.random.randint(key_list[4], (QUERIES, K), 0, 2)
    chosen_ids = jnp.where(use_fresh == 1, fresh_ids[picked], old_rows)
    flat_ids = chosen_ids.reshape(-1)
    corner = jax.random.randint(key_list[5], (2,), 0, QUERIES * K)
    flat_ids = flat_ids.at[corner[0]].set(INDEX_ROWS - 1)
    flat_ids = flat_ids.at[corner[1]].set(0)
    return flat_ids.reshape(QUERIES, K).astype(jnp.int32)


def index_values(key, low, high):
    key = jax.random.fold_in(key, 17)
    first_key, second_key = jax.random.split(key)
    base_draw = jnp.clip(jax.random.normal(first_key, (INDEX_ROWS, D), jnp.float32), -6.0, 6.0)
    row_scale = jnp.exp(jax.random.uniform(second_key, (INDEX_ROWS, 1), jnp.float32, math.log(low), math.log(high)))
    return base_draw * row_scale


def draw_passage_rows(key, part):
    return fresh_targets(key)


def draw_candidates(key, part):
    chosen_ids = candidate_table(key)
    return chosen_ids


def draw_old_index(key, part):
    old_table = index_values(key, 0.04, 0.08)
    return old_table.astype(jnp.bfloat16)


def draw_queries(key, part):
    key = jax.random.fold_in(key, 5)
    key_list = jax.random.split(key, 1)
    base_draw = jnp.clip(jax.random.normal(key_list[0], (QUERIES, D), jnp.float32), -4.0, 4.0) * 2.0
    return base_draw.astype(jnp.bfloat16)


def draw_teacher(key, part):
    key = jax.random.fold_in(key, 7)
    key_list = jax.random.split(key, 1)
    return jnp.clip(jax.random.normal(key_list[0], (QUERIES, K), jnp.float32) * 2.0, -8.0, 8.0)


def levels(own_key, shape, cuts, low, largest):
    loudness, own = 1.0, jax.random.fold_in(own_key, 6)
    for axis_at, blocks in cuts:
        draws = jnp.exp(jax.random.uniform(jax.random.fold_in(own, axis_at), (blocks,), jnp.float32, low / len(cuts), largest / len(cuts)))
        loudness = loudness * jnp.repeat(draws, shape[axis_at] // blocks).reshape([-1 if axis == axis_at else 1 for axis in range(len(shape))])
    return loudness


def scatter_about(rng, shape, width, reach, cuts=(), kind=jnp.bfloat16):
    factor_of = levels(rng, shape, cuts, -0.22, 0.18) if cuts else 1.0
    drawn = jax.random.normal(rng, shape, jnp.float32) * width * factor_of
    return jnp.minimum(jnp.maximum(drawn, -reach), reach).astype(kind)


def setup_inputs(seed: int = 0) -> dict:
    streams_of = jax.random.split(jax.random.key(seed), 10)
    hidden_states = scatter_about(streams_of[0], (PASSAGES * LEN, D), 1.0, 6.0, ((0, 128),))
    w_in = scatter_about(streams_of[1], (D, FF), D ** -0.5, 0.21875)
    w_out = scatter_about(streams_of[2], (FF, D), FF ** -0.5, 0.109375)
    ln_gain = jnp.clip(1.0 + 0.18 * jax.random.normal(streams_of[3], (D,), jnp.float32), 0.1, 1.9)
    passage_rows = draw_passage_rows(jax.random.fold_in(streams_of[9], 71), 0)
    old_index = draw_old_index(jax.random.fold_in(streams_of[9], 71), 0)
    queries = draw_queries(jax.random.fold_in(streams_of[9], 71), 0)
    candidates = draw_candidates(jax.random.fold_in(streams_of[9], 71), 0)
    teacher = draw_teacher(jax.random.fold_in(streams_of[9], 71), 0)
    return {"hidden_states": hidden_states, "w_in": w_in, "w_out": w_out, "ln_gain": ln_gain, "passage_rows": passage_rows, "old_index": old_index, "queries": queries, "candidates": candidates, "teacher": teacher}


epsilon = 1e-05

def encode_block(token_rows, w_in, w_out, ln_gain):
    inner_rows = jax.nn.gelu(jnp.dot(token_rows, w_in, preferred_element_type=jnp.float32), approximate=False).astype(jnp.bfloat16)
    mixed_rows = token_rows.astype(jnp.float32) + jnp.dot(inner_rows, w_out, preferred_element_type=jnp.float32)
    centered = mixed_rows - lax.optimization_barrier(jnp.mean(mixed_rows, axis=-1, keepdims=True))
    spread = lax.optimization_barrier(jnp.mean(centered * centered, axis=-1, keepdims=True))
    normed = centered * lax.rsqrt(spread + epsilon) * ln_gain.astype(jnp.float32)
    return lax.optimization_barrier(jnp.mean(normed.reshape(-1, LEN, D), axis=1)).astype(jnp.bfloat16)

def distill(scores, teacher):
    log_student = jax.nn.log_softmax(scores, axis=-1)
    log_teacher = jax.nn.log_softmax(teacher, axis=-1)
    weight_teacher = jnp.exp(log_teacher)
    loss_rows = lax.optimization_barrier(jnp.sum(weight_teacher * (log_teacher - log_student), axis=-1))
    weight_diff = (jnp.exp(log_student) - weight_teacher).astype(jnp.bfloat16)
    return (loss_rows, weight_diff)

def reference(hidden_states, w_in, w_out, ln_gain, passage_rows, old_index, queries, candidates, teacher):
    token_blocks = hidden_states.reshape(PASSAGES // 4, 4 * LEN, D)
    fresh_rows = lax.map(lambda block_rows: encode_block(block_rows, w_in, w_out, ln_gain), token_blocks).reshape(PASSAGES, D)
    new_index = old_index.at[passage_rows].set(fresh_rows)

    def score_block(inputs):
        query_block, cand_block, teacher_block = inputs
        cand_rows = new_index[cand_block].astype(jnp.float32)
        scores = jnp.einsum('qd,qkd->qk', query_block.astype(jnp.float32), cand_rows, precision=lax.Precision.HIGHEST)
        loss_rows, weight_diff = distill(scores, teacher_block)
        query_grad = jnp.einsum('qk,qkd->qd', weight_diff.astype(jnp.float32), cand_rows, precision=lax.Precision.HIGHEST)
        return (loss_rows, query_grad)
    block_size = math.gcd(QUERIES, 256)
    loss_rows, query_grad = lax.map(score_block, (queries.reshape(-1, block_size, D), candidates.reshape(-1, block_size, K), teacher.reshape(-1, block_size, K)))
    return (new_index, loss_rows.reshape(QUERIES), query_grad.reshape(QUERIES, D))
```

```python
import functools

import jax
import jax.numpy as jnp
from jax import lax
from jax.experimental import pallas as pl
from jax.experimental.pallas import tpu as pltpu
from jax.sharding import PartitionSpec as P

LEN = 256
EPS = 1e-05
MIB = 2**20
MESH = pl.DeviceIdType.MESH
BF16, F32, I32 = jnp.bfloat16, jnp.float32, jnp.int32
TAIL = 128
FLAG = 8192
NONE = -1e30


def gelu(v):
    return 0.5 * v * (1.0 + lax.erf(v * 0.7071067811865476))


def encode_kernel(block, chunk, shards, shard_rows, x_hbm, win_hbm, wout_hbm, gain_ref, rows_ref,
                  out_ref, x, win, wout, inner, mixed, fresh, slots, sem):
    tokens, d = x.shape
    ff = win.shape[1]
    blocks, chunks = tokens // block, ff // chunk
    jobs = [pltpu.make_async_copy(x_hbm, x, sem.at[0]),
            pltpu.make_async_copy(win_hbm, win, sem.at[1]),
            pltpu.make_async_copy(wout_hbm, wout, sem.at[2])]
    for job in jobs:
        job.start()
    for job in jobs:
        job.wait()

    def norm(b):
        for j in range(block // LEN):
            y = mixed[b % 2, j * LEN:(j + 1) * LEN, :]
            centered = y - jnp.mean(y, axis=-1, keepdims=True)
            spread = jnp.mean(centered * centered, axis=-1, keepdims=True)
            normed = centered * lax.rsqrt(spread + EPS)
            k = b * (block // LEN) + j
            fresh[k:k + 1, :] = jnp.sum(normed, axis=0, keepdims=True) * (1.0 / LEN) * gain_ref[...]

    for b in range(blocks):
        rows = slice(b * block, (b + 1) * block)
        for c in range(chunks):
            cols = slice(c * chunk, (c + 1) * chunk)
            h = jnp.dot(x[rows, :], win[:, cols], preferred_element_type=F32)
            inner[b % 2, :, cols] = gelu(h).astype(BF16)
            if c == 0 and b > 0:
                norm(b - 1)
        mixed[b % 2] = x[rows, :].astype(F32) + jnp.dot(
            inner[b % 2], wout[...], preferred_element_type=F32)
    norm(blocks - 1)

    passages = tokens // LEN
    ids = [rows_ref[p] for p in range(passages)]
    owner = [i // shard_rows for i in ids]
    lane = lax.broadcasted_iota(I32, (1, TAIL), 1)
    slot_iota = lax.broadcasted_iota(I32, (2 * shards, d + TAIL), 0)
    filled = jnp.zeros((2 * shards, d + TAIL), F32)
    for p in range(passages):
        rank = sum([(owner[q] == owner[p]).astype(I32) for q in range(p)], jnp.int32(0))
        place = owner[p] * 2 + rank
        local = ids[p] - owner[p] * shard_rows
        tail = jnp.where(lane == 0, local // 64, jnp.where(lane == 1, local % 64, jnp.where(lane == 2, 1, 0)))
        row = jnp.concatenate([fresh[p:p + 1, :], tail.astype(F32)], axis=1)
        filled = jnp.where(slot_iota == place, row, filled)
    slots[...] = filled.astype(BF16).astype(F32)
    for s in range(shards):
        out_ref[s] = slots[2 * s:2 * s + 2, :]


def encode(shards, shard_rows, hidden, w_in, w_out, gain, passage_rows):
    tokens, d = hidden.shape
    ff = w_in.shape[1]
    block, chunk = 512, 768
    anywhere = pl.BlockSpec(memory_space=pl.ANY)
    return pl.pallas_call(
        functools.partial(encode_kernel, block, chunk, shards, shard_rows),
        out_shape=jax.ShapeDtypeStruct((shards, 2, d + TAIL), F32),
        in_specs=[anywhere] * 3 + [pl.BlockSpec(memory_space=pltpu.VMEM), pl.BlockSpec(memory_space=pltpu.SMEM)],
        out_specs=pl.BlockSpec(memory_space=pltpu.VMEM),
        scratch_shapes=[
            pltpu.VMEM((tokens, d), BF16),
            pltpu.VMEM((d, ff), BF16),
            pltpu.VMEM((ff, d), BF16),
            pltpu.VMEM((2, block, ff), BF16),
            pltpu.VMEM((2, block, d), F32),
            pltpu.VMEM((tokens // LEN, d), F32),
            pltpu.VMEM((2 * shards, d + TAIL), F32),
            pltpu.SemaphoreType.DMA((3,)),
        ],
        compiler_params=pltpu.CompilerParams(vmem_limit_bytes=56 * MIB),
        name="encode",
    )(hidden, w_in, w_out, gain.reshape(1, d), passage_rows)


def exchange_kernel(loaders, shards, slots_ref, out_ref, mine, packed, send1, recv1, send2, recv2):
    li, si = lax.axis_index("loader"), lax.axis_index("shard")
    barrier = pltpu.get_barrier_semaphore()
    for k in range(1, shards):
        pl.semaphore_signal(barrier, inc=1, device_id=(li, lax.rem(si + k, shards)), device_id_type=MESH)
    for k in range(1, loaders):
        pl.semaphore_signal(barrier, inc=1, device_id=(lax.rem(li + k, loaders), si), device_id_type=MESH)
    pl.semaphore_wait(barrier, shards + loaders - 2)
    first = []
    for k in range(1, shards):
        to = lax.rem(si + k, shards)
        copy = pltpu.make_async_remote_copy(
            src_ref=slots_ref.at[to], dst_ref=mine.at[si], send_sem=send1.at[k], recv_sem=recv1.at[k],
            device_id=(li, to), device_id_type=MESH)
        copy.start()
        first.append(copy)
    mine[si] = slots_ref[si]
    for copy in first:
        copy.wait_recv()
    for s in range(shards):
        packed[2 * s:2 * s + 2, :] = mine[s]
    out_ref[li] = packed[...].astype(BF16)
    second = []
    for k in range(1, loaders):
        copy = pltpu.make_async_remote_copy(
            src_ref=out_ref.at[li], dst_ref=out_ref.at[li], send_sem=send2.at[k], recv_sem=recv2.at[k],
            device_id=(lax.rem(li + k, loaders), si), device_id_type=MESH)
        copy.start()
        second.append(copy)
    for copy in second:
        copy.wait_recv()
    for copy in first + second:
        copy.wait_send()


def exchange(loaders, shards, slots):
    width = slots.shape[-1]
    return pl.pallas_call(
        functools.partial(exchange_kernel, loaders, shards),
        out_shape=jax.ShapeDtypeStruct((loaders, 2 * shards, width), BF16),
        in_specs=[pl.BlockSpec(memory_space=pltpu.VMEM)],
        out_specs=pl.BlockSpec(memory_space=pltpu.VMEM),
        scratch_shapes=[
            pltpu.VMEM((shards, 2, width), F32),
            pltpu.VMEM((2 * shards, width), F32),
            pltpu.SemaphoreType.DMA((shards,)),
            pltpu.SemaphoreType.DMA((shards,)),
            pltpu.SemaphoreType.DMA((loaders,)),
            pltpu.SemaphoreType.DMA((loaders,)),
        ],
        compiler_params=pltpu.CompilerParams(collective_id=0, has_side_effects=True),
        name="exchange",
    )(slots)


def both_halves(x):
    return jnp.concatenate([x, x], axis=1)


def score_kernel(tile, fresh_ref, q_ref, cand_ref, teacher_ref, old_hbm,
                 new_hbm, score_ref, stats_ref, old, new, s_all, hi_s, lo_s, got, in_sem, out_sem):
    rows, d = old.shape
    nq = q_ref.shape[0]
    k = cand_ref.shape[0]
    tiles = rows // tile
    loads = [pltpu.make_async_copy(old_hbm.at[pl.ds(t * tile, tile)], old.at[pl.ds(t * tile, tile)], in_sem.at[t])
             for t in range(tiles)]
    for load in loads:
        load.start()
    base = lax.axis_index("shard") * rows
    local = cand_ref[...] - base
    local_q = jnp.concatenate([local, local], axis=0).T
    hi_s[...] = local_q >> 7
    lo_s[...] = local_q & 127

    lane = lax.broadcasted_iota(I32, (8, TAIL), 1)
    digits = jnp.where(lane == 0, 64.0, jnp.where(lane == 1, 1.0, jnp.where(lane == 2, float(FLAG), 0.0))).astype(BF16)
    where_to = lax.dot_general(digits, fresh_ref[:, d:d + TAIL], (((1,), (1,)), ((), ())),
                               preferred_element_type=F32)[0:1, :].astype(I32)
    slots = fresh_ref.shape[0]
    ones = jnp.ones((slots, 128), BF16)
    row_iota = lax.broadcasted_iota(I32, (tile, slots), 0)
    stores = []
    for t in range(tiles):
        rs = slice(t * tile, (t + 1) * tile)
        place = jnp.where(row_iota + (t * tile + FLAG) == where_to, 1.0, 0.0).astype(BF16)
        put = jnp.dot(place, fresh_ref[:, 0:d], preferred_element_type=F32)
        has = jnp.dot(place, ones, preferred_element_type=F32)
        loads[t].wait()
        for c in range(d // 128):
            cs = slice(c * 128, (c + 1) * 128)
            new[rs, cs] = jnp.where(has > 0.5, put[:, cs], old[rs, cs].astype(F32)).astype(BF16)
        store = pltpu.make_async_copy(new.at[pl.ds(t * tile, tile)], new_hbm.at[pl.ds(t * tile, tile)], out_sem.at[t])
        store.start()
        stores.append(store)
        s_all[:, rs] = lax.dot_general(q_ref[...], new[rs, :], (((1,), (1,)), ((), ())), preferred_element_type=F32)

    def pick(g, carry):
        qs = pl.ds(pl.multiple_of(g * 8, 8), 8)
        hi, lo = hi_s[qs, :], lo_s[qs, :]
        out = jnp.zeros((8, 128), F32)
        for h in range(rows // 128):
            got_h = jnp.take_along_axis(s_all[qs, h * 128:(h + 1) * 128], lo, axis=1, mode="promise_in_bounds")
            out = jnp.where(hi == h, got_h, out)
        got[qs, :] = out
        return carry

    lax.fori_loop(0, nq // 8, pick, 0)
    score = got[...].T[0:k, :]
    owned = (local >= 0) & (local < rows)
    score_ref[...] = score
    teacher = teacher_ref[...]
    shifted = teacher - jnp.max(teacher, axis=0, keepdims=True)
    log_t = shifted - jnp.log(jnp.sum(jnp.exp(shifted), axis=0, keepdims=True))
    p_t = jnp.exp(log_t)
    top = jnp.max(jnp.where(owned, score, NONE), axis=0, keepdims=True)
    diff = score - top
    z = jnp.sum(jnp.where(owned, jnp.exp(jnp.where(owned, diff, 0.0)), 0.0), axis=0, keepdims=True)
    a = jnp.sum(jnp.where(owned, p_t * diff, 0.0), axis=0, keepdims=True)
    b = jnp.sum(jnp.where(owned, p_t, 0.0), axis=0, keepdims=True)
    e = jnp.sum(p_t * log_t, axis=0, keepdims=True)
    stats_ref[...] = jnp.concatenate([top, z, a, b, e, e, e, e], axis=0)
    for store in stores:
        store.wait()


def score(fresh, queries, cand_t, teacher_t, old_index):
    rows, d = old_index.shape
    nq = queries.shape[0]
    k = cand_t.shape[0]
    tile = 512
    anywhere = pl.BlockSpec(memory_space=pl.ANY)
    vmem = pl.BlockSpec(memory_space=pltpu.VMEM)
    return pl.pallas_call(
        functools.partial(score_kernel, tile),
        out_shape=[
            jax.ShapeDtypeStruct((rows, d), BF16),
            jax.ShapeDtypeStruct((k, nq), F32),
            jax.ShapeDtypeStruct((8, nq), F32),
        ],
        in_specs=[vmem] * 4 + [anywhere],
        out_specs=[anywhere, vmem, vmem],
        scratch_shapes=[
            pltpu.VMEM((rows, d), BF16),
            pltpu.VMEM((rows, d), BF16),
            pltpu.VMEM((nq, rows), F32),
            pltpu.VMEM((nq, 2 * k), I32),
            pltpu.VMEM((nq, 2 * k), I32),
            pltpu.VMEM((nq, 2 * k), F32),
            pltpu.SemaphoreType.DMA((rows // tile,)),
            pltpu.SemaphoreType.DMA((rows // tile,)),
        ],
        compiler_params=pltpu.CompilerParams(vmem_limit_bytes=56 * MIB),
        name="score",
    )(fresh, queries, cand_t, teacher_t, old_index)


def grad_kernel(shards, score_ref, stats_ref, cand_ref, teacher_ref, new_hbm, loss_ref, grad_ref,
                new, stats, w_s, hi_s, lo_s, spread, part, own, inbox,
                load_sem, send1, recv1, send2, recv2):
    rows, d = new.shape
    k, nq = score_ref.shape
    per = nq // shards
    li, si = lax.axis_index("loader"), lax.axis_index("shard")
    load = pltpu.make_async_copy(new_hbm, new, load_sem)
    load.start()
    barrier = pltpu.get_barrier_semaphore()
    for j in range(1, shards):
        pl.semaphore_signal(barrier, inc=1, device_id=(li, lax.rem(si + j, shards)), device_id_type=MESH)
    pl.semaphore_wait(barrier, shards - 1)
    first = []
    for j in range(1, shards):
        copy = pltpu.make_async_remote_copy(
            src_ref=stats_ref, dst_ref=stats.at[si], send_sem=send1.at[j], recv_sem=recv1.at[j],
            device_id=(li, lax.rem(si + j, shards)), device_id_type=MESH)
        copy.start()
        first.append(copy)
    stats[si] = stats_ref[...]

    local = cand_ref[...] - si * rows
    owned = (local >= 0) & (local < rows)
    local_q = jnp.concatenate([local, local], axis=0).T
    hi_s[...] = local_q >> 7
    lo_s[...] = (local_q & 127).astype(F32)
    teacher = teacher_ref[...]
    shifted = teacher - jnp.max(teacher, axis=0, keepdims=True)
    p_t = jnp.exp(shifted - jnp.log(jnp.sum(jnp.exp(shifted), axis=0, keepdims=True)))
    for copy in first:
        copy.wait_recv()
    every = [stats[s] for s in range(shards)]
    top = functools.reduce(jnp.maximum, [e[0:1] for e in every])
    z = sum([e[1:2] * jnp.exp(e[0:1] - top) for e in every])
    cross = sum([e[2:3] + e[3:4] * (e[0:1] - top) for e in every])
    log_z = jnp.log(z)
    loss = stats_ref[4:5, :] - cross + log_z
    out = jnp.zeros((1, per), F32)
    for s in range(shards):
        out = jnp.where(si == s, loss[:, s * per:(s + 1) * per], out)
    loss_ref[...] = out
    student = jnp.exp(jnp.where(owned, score_ref[...] - top - log_z, 0.0))
    weight = jnp.where(owned, student - p_t, 0.0).astype(BF16).astype(F32)
    w_s[...] = jnp.concatenate([weight, weight], axis=0).T

    lane = lax.broadcasted_iota(I32, (8, 2 * k), 1)
    sub = lax.broadcasted_iota(I32, (8, 2 * k), 0)
    masks = [lane // k + 2 * v == sub for v in range(4)]
    lo_iota = lax.broadcasted_iota(I32, (128, 8 * k), 0).astype(F32)
    his = rows // 128

    def group(q0):
        qs = pl.ds(pl.multiple_of(q0, 8), 8)
        w2, hi2, lo2 = w_s[qs, :], hi_s[qs, :], lo_s[qs, :]
        wide = jnp.concatenate([jnp.where(m, w2, 0.0) for m in masks], axis=1)
        low = jnp.concatenate(
            [jnp.sum(jnp.where(m, lo2, 0.0), axis=0, keepdims=True) for m in masks], axis=1)
        hi_wide = jnp.concatenate([hi2] * 4, axis=1)
        left = jnp.concatenate([jnp.where(hi_wide == h, wide, 0.0) for h in range(his)], axis=0).astype(BF16)
        right = jnp.where(lo_iota == low, 1.0, 0.0).astype(BF16)
        return lax.dot_general(left, right, (((1,), (1,)), ((), ())), preferred_element_type=F32)

    def place(g, carry):
        one, two = group(g * 16), group(g * 16 + 8)
        qs = pl.ds(pl.multiple_of(g * 16, 16), 16)
        for h in range(his):
            both = jnp.concatenate([one[h * 8:(h + 1) * 8], two[h * 8:(h + 1) * 8]], axis=0)
            spread[qs, h * 128:(h + 1) * 128] = both.astype(BF16)
        return carry

    lax.fori_loop(0, nq // 16, place, 0)
    load.wait()
    total = jnp.dot(spread[...], new[...], preferred_element_type=F32)
    mine = jnp.zeros((per, d), F32)
    for s in range(shards):
        block = total[s * per:(s + 1) * per, :]
        part[s] = block.astype(BF16)
        mine = jnp.where(si == s, block, mine)
    own[...] = mine
    second = []
    for j in range(1, shards):
        to = lax.rem(si + j, shards)
        copy = pltpu.make_async_remote_copy(
            src_ref=part.at[to], dst_ref=inbox.at[j], send_sem=send2.at[j], recv_sem=recv2.at[j],
            device_id=(li, to), device_id_type=MESH)
        copy.start()
        second.append(copy)
    got = own[...]
    for j, copy in enumerate(second):
        copy.wait_recv()
        got = got + inbox[j + 1].astype(F32)
    grad_ref[...] = got
    for copy in first + second:
        copy.wait_send()


def gradient(shards, scores, stats, cand_t, teacher_t, new_index):
    rows, d = new_index.shape
    k, nq = scores.shape
    per = nq // shards
    vmem = pl.BlockSpec(memory_space=pltpu.VMEM)
    return pl.pallas_call(
        functools.partial(grad_kernel, shards),
        out_shape=[jax.ShapeDtypeStruct((1, per), F32), jax.ShapeDtypeStruct((per, d), F32)],
        in_specs=[vmem] * 4 + [pl.BlockSpec(memory_space=pl.ANY)],
        out_specs=[vmem, vmem],
        scratch_shapes=[
            pltpu.VMEM((rows, d), BF16),
            pltpu.VMEM((shards, 8, nq), F32),
            pltpu.VMEM((nq, 2 * k), F32),
            pltpu.VMEM((nq, 2 * k), I32),
            pltpu.VMEM((nq, 2 * k), F32),
            pltpu.VMEM((nq, rows), BF16),
            pltpu.VMEM((shards, per, d), BF16),
            pltpu.VMEM((per, d), F32),
            pltpu.VMEM((shards, per, d), BF16),
            pltpu.SemaphoreType.DMA,
            pltpu.SemaphoreType.DMA((shards,)),
            pltpu.SemaphoreType.DMA((shards,)),
            pltpu.SemaphoreType.DMA((shards,)),
            pltpu.SemaphoreType.DMA((shards,)),
        ],
        compiler_params=pltpu.CompilerParams(collective_id=1, has_side_effects=True, vmem_limit_bytes=56 * MIB),
        name="gradient",
    )(scores, stats, cand_t, teacher_t, new_index)


def solution(mesh):
    loaders, shards = mesh.shape["loader"], mesh.shape["shard"]

    def local(hidden_states, w_in, w_out, ln_gain, passage_rows, old_index, queries, candidates, teacher):
        cand_t, teacher_t = candidates.T, teacher.T
        slots = encode(shards, old_index.shape[0], hidden_states, w_in, w_out, ln_gain, passage_rows)
        fresh = exchange(loaders, shards, slots)
        fresh = fresh.reshape(loaders * 2 * shards, fresh.shape[-1])
        new_index, scores, stats = score(fresh, queries, cand_t, teacher_t, old_index)
        loss, grad = gradient(shards, scores, stats, cand_t, teacher_t, new_index)
        return new_index, loss.reshape(-1), grad

    return jax.shard_map(
        local,
        mesh=mesh,
        in_specs=(
            P(("loader", "shard"), None),
            P(),
            P(),
            P(),
            P(("loader", "shard")),
            P("shard", None),
            P("loader", None),
            P("loader", None),
            P("loader", None),
        ),
        out_specs=(P("shard", None), P(("loader", "shard")), P(("loader", "shard"), None)),
        check_vma=False,
    )
```

```python
import functools

import jax
import jax.numpy as jnp
from jax import lax
from jax.experimental import pallas as pl
from jax.experimental.pallas import tpu as pltpu
from jax.sharding import PartitionSpec as P

LEN = 256
EPS = 1e-05
MIB = 2**20
MESH = pl.DeviceIdType.MESH
BF16, F32, I32 = jnp.bfloat16, jnp.float32, jnp.int32
NONE = -1e30


def gelu(v):
    return 0.5 * v * (1.0 + lax.erf(v * 0.7071067811865476))


def main_kernel(block, chunk, loaders, shards,
                x_hbm, win_hbm, wout_hbm, gain_ref, rows_ref, old_hbm, q_ref, cand_ref, teacher_ref,
                loss_ref, grad_ref, fresh_ref, place_ref,
                x, win, wout, inner, mixed, fresh, old, s_all, a_s, hi_s, lo_s, t_map, got, flat, spread, w_s,
                ids, ids_a, ids_b, slots, mine, packed, stats, part, own, inbox,
                load_sem, ids1_send, ids1_recv, ids2_send, ids2_recv,
                send1, recv1, send2, recv2, send3, recv3, send4, recv4):
    tokens, d = x.shape
    ff = win.shape[1]
    rows = old.shape[0]
    k, nq = cand_ref.shape
    per = nq // shards
    blocks, chunks = tokens // block, ff // chunk
    his = rows // 128
    places = loaders * 2 * shards
    ext = his + places // 128
    li, si = lax.axis_index("loader"), lax.axis_index("shard")
    shard_peers = [(li, lax.rem(si + j, shards)) for j in range(1, shards)]
    loader_peers = [(lax.rem(li + j, loaders), si) for j in range(1, loaders)]

    jobs = [pltpu.make_async_copy(src, dst, load_sem.at[i]) for i, (src, dst) in enumerate(
        [(x_hbm, x), (win_hbm, win), (wout_hbm, wout), (old_hbm, old)])]
    for job in jobs[:3]:
        job.start()
    barrier = pltpu.get_barrier_semaphore()
    for peer in shard_peers + loader_peers:
        pl.semaphore_signal(barrier, inc=1, device_id=peer, device_id_type=MESH)

    def send(src, dst, sends, recvs, peers):
        copies = []
        for j, peer in enumerate(peers):
            copy = pltpu.make_async_remote_copy(
                src_ref=src(peer), dst_ref=dst, send_sem=sends.at[j], recv_sem=recvs.at[j],
                device_id=peer, device_id_type=MESH)
            copy.start()
            copies.append(copy)
        return copies

    def arrive(copies):
        for copy in copies:
            copy.wait_recv()

    started = []

    def norm(b):
        for j in range(block // LEN):
            y = mixed[b % 2, j * LEN:(j + 1) * LEN, :]
            centered = y - jnp.mean(y, axis=-1, keepdims=True)
            var = jnp.mean(centered * centered, axis=-1, keepdims=True)
            normed = centered * lax.rsqrt(var + EPS)
            n = b * (block // LEN) + j
            fresh[n:n + 1, :] = jnp.sum(normed, axis=0, keepdims=True) * (1.0 / LEN) * gain_ref[...].reshape(1, d)

    def encode_block(b):
        rs = slice(b * block, (b + 1) * block)
        for c in range(chunks):
            cs = slice(c * chunk, (c + 1) * chunk)
            h = jnp.dot(x[rs, :], win[:, cs], preferred_element_type=F32)
            inner[b % 2, :, cs] = gelu(h).astype(BF16)
            if c == 0 and b > 0:
                norm(b - 1)
        mixed[b % 2] = x[rs, :].astype(F32) + jnp.dot(inner[b % 2], wout[...], preferred_element_type=F32)

    for job in jobs[:3]:
        job.wait()
    jobs[3].start()
    encode_block(0)

    passages = tokens // LEN
    lane8 = lax.broadcasted_iota(I32, (8, 128), 1)
    numbers = [rows_ref[p] for p in range(passages)]
    block_ids = jnp.full((8, 128), -1, I32)
    for p in range(passages):
        block_ids = jnp.where(lane8 == p, numbers[p], block_ids)
    ids[...] = block_ids
    pl.semaphore_wait(barrier, shards + loaders - 2)
    ids_a[si] = block_ids
    sent = send(lambda peer: ids, ids_a.at[si], ids1_send, ids1_recv, shard_peers)
    started += sent
    encode_block(1)
    arrive(sent)
    seen = jnp.concatenate([ids_a[s, 0:1, :] for s in range(shards)], axis=0)
    mine_mask = (seen >= si * rows) & (seen < (si + 1) * rows)
    lane_f = lane8.astype(F32)
    value = (seen - si * rows).astype(F32)
    at0 = jnp.min(jnp.where(mine_mask, lane_f, 999.0), axis=1, keepdims=True)
    at1 = jnp.min(jnp.where(mine_mask & (lane_f != at0), lane_f, 999.0), axis=1, keepdims=True)
    for r, at in enumerate((at0, at1)):
        found = jnp.sum(jnp.where(lane_f == at, value, 0.0), axis=1, keepdims=True)
        ids_b[li, r * shards:(r + 1) * shards, :] = jnp.broadcast_to(jnp.where(at < 900.0, found, -1.0), (8, 128))
    sent = send(lambda peer: ids_b.at[li], ids_b.at[li], ids2_send, ids2_recv, loader_peers)
    started += sent
    for b in range(2, blocks):
        encode_block(b)
    norm(blocks - 1)

    owner = [i // rows for i in numbers]
    slot_iota = lax.broadcasted_iota(I32, (2 * shards, d), 0)
    filled = jnp.zeros((2 * shards, d), F32)
    for p in range(passages):
        rank = sum([(owner[o] == owner[p]).astype(I32) for o in range(p)], jnp.int32(0))
        filled = jnp.where(slot_iota == owner[p] * 2 + rank, fresh[p:p + 1, :], filled)
    for s in range(shards):
        slots[s] = filled[2 * s:2 * s + 2, :]
    mine[si] = slots[si]
    sent_a = send(lambda peer: slots.at[peer[1]], mine.at[si], send1, recv1, shard_peers)
    started += sent_a

    jobs[3].wait()
    tile = 512
    for t in range(rows // tile):
        rs = slice(t * tile, (t + 1) * tile)
        s_all[:, rs] = lax.dot_general(q_ref[...], old[rs, :], (((1,), (1,)), ((), ())), preferred_element_type=F32)

    arrive(sent_a)
    for s in range(shards):
        for r in range(2):
            packed[r * shards + s:r * shards + s + 1, :] = mine[s, r:r + 1, :]
    fresh_ref[li] = packed[...].astype(BF16)
    sent_b = send(lambda peer: fresh_ref.at[li], fresh_ref.at[li], send2, recv2, loader_peers)
    started += sent_b

    arrive(sent)
    where_to = ids_b[...].reshape(places, 128).T[0:8, :]
    place_ref[...] = where_to
    place_i = where_to[0:1, :].astype(I32)
    left = jnp.where(lax.broadcasted_iota(I32, (his, places), 0) == (place_i >> 7),
                     (lax.broadcasted_iota(I32, (his, places), 1) + 1).astype(F32), 0.0).astype(BF16)
    right = jnp.where(lax.broadcasted_iota(I32, (128, places), 0) == (place_i & 127), 1.0, 0.0).astype(BF16)
    t_map[...] = lax.dot_general(left, right, (((1,), (1,)), ((), ())), preferred_element_type=F32)

    local = cand_ref[...] - si * rows
    owned = (local >= 0) & (local < rows)
    high = jnp.where(owned, local >> 7, -1)
    low = local & 127
    hi_s[...] = jnp.concatenate([high, high], axis=0).T
    lo_s[...] = jnp.concatenate([low, low], axis=0).T

    lane = lax.broadcasted_iota(I32, (8, 2 * k), 1)
    sub = lax.broadcasted_iota(I32, (8, 2 * k), 0)
    masks = [lane // k + 2 * v == sub for v in range(4)]

    def pick(g, carry):
        qs = pl.ds(pl.multiple_of(g * 8, 8), 8)
        hi, lo = hi_s[qs, :], lo_s[qs, :]
        out = jnp.zeros((8, 128), F32)
        spot = jnp.zeros((8, 128), F32)
        for h in range(his):
            here = hi == h
            out = jnp.where(here, jnp.take_along_axis(
                s_all[qs, h * 128:(h + 1) * 128], lo, axis=1, mode="promise_in_bounds"), out)
            spot = jnp.where(here, jnp.take_along_axis(
                jnp.broadcast_to(t_map[h:h + 1, :], (8, 128)), lo, axis=1, mode="promise_in_bounds"), spot)
        is_fresh = spot > 0.5
        slot = spot.astype(I32) - 1
        hi = jnp.where(is_fresh, his + (slot >> 7), hi)
        lo = jnp.where(is_fresh, slot & 127, lo)
        hi_s[qs, :] = hi
        lo_s[qs, :] = lo
        got[qs, :] = out
        lo_f = lo.astype(F32)
        flat[g] = jnp.broadcast_to(jnp.concatenate(
            [jnp.sum(jnp.where(m, lo_f, 0.0), axis=0, keepdims=True) for m in masks], axis=1), (8, 8 * k))
        wide = jnp.concatenate([jnp.where(m, hi, -1) for m in masks], axis=1)
        a_s[g] = jnp.concatenate([jnp.where(wide == h, 1.0, 0.0) for h in range(ext)], axis=0).astype(BF16)
        return carry

    lax.fori_loop(0, nq // 8, pick, 0)
    teacher = teacher_ref[...]
    shifted = teacher - jnp.max(teacher, axis=0, keepdims=True)
    log_t = shifted - jnp.log(jnp.sum(jnp.exp(shifted), axis=0, keepdims=True))
    p_t = jnp.exp(log_t)
    entropy = jnp.sum(p_t * log_t, axis=0, keepdims=True)

    arrive(sent_b)
    rows_f = fresh_ref[...].reshape(places, d)
    s_fresh = lax.dot_general(q_ref[...], rows_f, (((1,), (1,)), ((), ())), preferred_element_type=F32)
    s_all[:, 0:places] = s_fresh

    def pick_fresh(g, carry):
        qs = pl.ds(pl.multiple_of(g * 8, 8), 8)
        hi, lo = hi_s[qs, :], lo_s[qs, :]
        out = got[qs, :]
        for h in range(places // 128):
            out = jnp.where(hi == his + h, jnp.take_along_axis(
                s_all[qs, h * 128:(h + 1) * 128], lo, axis=1, mode="promise_in_bounds"), out)
        got[qs, :] = out
        return carry

    lax.fori_loop(0, nq // 8, pick_fresh, 0)
    score = got[...].T[0:k, :]
    top = jnp.max(jnp.where(owned, score, NONE), axis=0, keepdims=True)
    diff = score - top
    z = jnp.sum(jnp.where(owned, jnp.exp(jnp.where(owned, diff, 0.0)), 0.0), axis=0, keepdims=True)
    a = jnp.sum(jnp.where(owned, p_t * diff, 0.0), axis=0, keepdims=True)
    b = jnp.sum(jnp.where(owned, p_t, 0.0), axis=0, keepdims=True)
    stats[si] = jnp.concatenate([top, z, a, b, top, z, a, b], axis=0)
    sent_s = send(lambda peer: stats.at[si], stats.at[si], send3, recv3, shard_peers)
    started += sent_s
    arrive(sent_s)
    every = [stats[s] for s in range(shards)]
    top = functools.reduce(jnp.maximum, [e[0:1] for e in every])
    z = sum([e[1:2] * jnp.exp(e[0:1] - top) for e in every])
    cross = sum([e[2:3] + e[3:4] * (e[0:1] - top) for e in every])
    log_z = jnp.log(z)
    loss = entropy - cross + log_z
    out = jnp.zeros((1, per), F32)
    for s in range(shards):
        out = jnp.where(si == s, loss[:, s * per:(s + 1) * per], out)
    loss_ref[...] = out
    student = jnp.exp(jnp.where(owned, score - top - log_z, 0.0))
    weight = jnp.where(owned, student - p_t, 0.0).astype(BF16).astype(F32)
    w_s[...] = jnp.concatenate([weight, weight], axis=0).T

    lo_iota = lax.broadcasted_iota(I32, (128, 8 * k), 0).astype(F32)

    def group(g):
        w2 = w_s[pl.ds(pl.multiple_of(g * 8, 8), 8), :]
        w_flat = jnp.concatenate(
            [jnp.sum(jnp.where(m, w2, 0.0), axis=0, keepdims=True) for m in masks], axis=1)
        right = jnp.where(lo_iota == flat[g][0:1, :], w_flat, 0.0).astype(BF16)
        return lax.dot_general(a_s[g], right, (((1,), (1,)), ((), ())), preferred_element_type=F32)

    def place(g, carry):
        one, two = group(g * 2), group(g * 2 + 1)
        qs = pl.ds(pl.multiple_of(g * 16, 16), 16)
        for h in range(ext):
            both = jnp.concatenate([one[h * 8:(h + 1) * 8], two[h * 8:(h + 1) * 8]], axis=0)
            spread[qs, h * 128:(h + 1) * 128] = both.astype(BF16)
        return carry

    lax.fori_loop(0, nq // 16, place, 0)
    total = (jnp.dot(spread[:, 0:rows], old[...], preferred_element_type=F32)
             + jnp.dot(spread[:, rows:rows + places], fresh_ref[...].reshape(places, d), preferred_element_type=F32))
    own_block = jnp.zeros((per, d), F32)
    for s in range(shards):
        piece = total[s * per:(s + 1) * per, :]
        part[s] = piece.astype(BF16)
        own_block = jnp.where(si == s, piece, own_block)
    own[...] = own_block
    sent_g = []
    for j, peer in enumerate(shard_peers):
        copy = pltpu.make_async_remote_copy(
            src_ref=part.at[peer[1]], dst_ref=inbox.at[j], send_sem=send4.at[j], recv_sem=recv4.at[j],
            device_id=peer, device_id_type=MESH)
        copy.start()
        sent_g.append(copy)
    acc = own[...]
    for j, copy in enumerate(sent_g):
        copy.wait_recv()
        acc = acc + inbox[j].astype(F32)
    grad_ref[...] = acc
    for copy in started + sent_g:
        copy.wait_send()


def main(loaders, shards, hidden, w_in, w_out, gain, passage_rows, old_index, queries, cand_t, teacher_t):
    tokens, d = hidden.shape
    ff = w_in.shape[1]
    rows = old_index.shape[0]
    k, nq = cand_t.shape
    per = nq // shards
    places = loaders * 2 * shards
    ext = (rows + places) // 128
    block, chunk = 512, 768
    anywhere = pl.BlockSpec(memory_space=pl.ANY)
    vmem = pl.BlockSpec(memory_space=pltpu.VMEM)
    smem = pl.BlockSpec(memory_space=pltpu.SMEM)
    dma = pltpu.SemaphoreType.DMA
    return pl.pallas_call(
        functools.partial(main_kernel, block, chunk, loaders, shards),
        out_shape=[
            jax.ShapeDtypeStruct((1, per), F32),
            jax.ShapeDtypeStruct((per, d), F32),
            jax.ShapeDtypeStruct((loaders, 2 * shards, d), BF16),
            jax.ShapeDtypeStruct((8, places), F32),
        ],
        in_specs=[anywhere] * 3 + [vmem, smem, anywhere, vmem, vmem, vmem],
        out_specs=[vmem] * 4,
        scratch_shapes=[
            pltpu.VMEM((tokens, d), BF16),
            pltpu.VMEM((d, ff), BF16),
            pltpu.VMEM((ff, d), BF16),
            pltpu.VMEM((2, block, ff), BF16),
            pltpu.VMEM((2, block, d), F32),
            pltpu.VMEM((tokens // LEN, d), F32),
            pltpu.VMEM((rows, d), BF16),
            pltpu.VMEM((nq, rows), F32),
            pltpu.VMEM((nq // 8, 8 * ext, 8 * k), BF16),
            pltpu.VMEM((nq, 2 * k), I32),
            pltpu.VMEM((nq, 2 * k), I32),
            pltpu.VMEM((rows // 128, 128), F32),
            pltpu.VMEM((nq, 2 * k), F32),
            pltpu.VMEM((nq // 8, 8, 8 * k), F32),
            pltpu.VMEM((nq, 128 * ext), BF16),
            pltpu.VMEM((nq, 2 * k), F32),
            pltpu.VMEM((8, 128), I32),
            pltpu.VMEM((shards, 8, 128), I32),
            pltpu.VMEM((loaders, 2 * shards, 128), F32),
            pltpu.VMEM((shards, 2, d), F32),
            pltpu.VMEM((shards, 2, d), F32),
            pltpu.VMEM((2 * shards, d), F32),
            pltpu.VMEM((shards, 8, nq), F32),
            pltpu.VMEM((shards, per, d), BF16),
            pltpu.VMEM((per, d), F32),
            pltpu.VMEM((shards, per, d), BF16),
            dma((4,)),
            dma((shards,)), dma((shards,)), dma((loaders,)), dma((loaders,)),
            dma((shards,)), dma((shards,)), dma((loaders,)), dma((loaders,)),
            dma((shards,)), dma((shards,)), dma((shards,)), dma((shards,)),
        ],
        compiler_params=pltpu.CompilerParams(collective_id=0, has_side_effects=True, vmem_limit_bytes=60 * MIB),
        name="main",
    )(hidden, w_in, w_out, gain, passage_rows, old_index, queries, cand_t, teacher_t)


def index_kernel(tile, fresh_ref, place_ref, loss_in, grad_in, old_hbm, new_hbm, loss_out, grad_out,
                 old, new, in_sem, out_sem):
    rows, d = old.shape
    tiles = rows // tile
    loads = [pltpu.make_async_copy(old_hbm.at[pl.ds(t * tile, tile)], old.at[pl.ds(t * tile, tile)], in_sem.at[t])
             for t in range(tiles)]
    for load in loads:
        load.start()
    loss_out[...] = loss_in[...]
    grad_out[...] = grad_in[...]
    where_to = place_ref[0:1, :].astype(I32)
    places = fresh_ref.shape[0]
    ones = jnp.ones((places, 128), BF16)
    row_iota = lax.broadcasted_iota(I32, (tile, places), 0)
    stores = []
    for t in range(tiles):
        rs = slice(t * tile, (t + 1) * tile)
        place = jnp.where(row_iota + t * tile == where_to, 1.0, 0.0).astype(BF16)
        put = jnp.dot(place, fresh_ref[...], preferred_element_type=F32)
        has = jnp.dot(place, ones, preferred_element_type=F32)
        loads[t].wait()
        for c in range(d // 128):
            cs = slice(c * 128, (c + 1) * 128)
            new[rs, cs] = jnp.where(has > 0.5, put[:, cs], old[rs, cs].astype(F32)).astype(BF16)
        store = pltpu.make_async_copy(new.at[pl.ds(t * tile, tile)], new_hbm.at[pl.ds(t * tile, tile)], out_sem.at[t])
        store.start()
        stores.append(store)
    for store in stores:
        store.wait()


def refresh(fresh, places, loss, grad, old_index):
    rows, d = old_index.shape
    tile = 512
    anywhere = pl.BlockSpec(memory_space=pl.ANY)
    vmem = pl.BlockSpec(memory_space=pltpu.VMEM)
    return pl.pallas_call(
        functools.partial(index_kernel, tile),
        out_shape=[jax.ShapeDtypeStruct((rows, d), BF16), jax.ShapeDtypeStruct(loss.shape, F32),
                   jax.ShapeDtypeStruct(grad.shape, F32)],
        in_specs=[vmem] * 4 + [anywhere],
        out_specs=[anywhere, vmem, vmem],
        scratch_shapes=[
            pltpu.VMEM((rows, d), BF16),
            pltpu.VMEM((rows, d), BF16),
            pltpu.SemaphoreType.DMA((rows // tile,)),
            pltpu.SemaphoreType.DMA((rows // tile,)),
        ],
        compiler_params=pltpu.CompilerParams(vmem_limit_bytes=48 * MIB),
        name="refresh",
    )(fresh, places, loss, grad, old_index)


def solution(mesh):
    loaders, shards = mesh.shape["loader"], mesh.shape["shard"]

    def local(hidden_states, w_in, w_out, ln_gain, passage_rows, old_index, queries, candidates, teacher):
        cand_t, teacher_t = candidates.T, teacher.T
        loss, grad, fresh, places = main(
            loaders, shards, hidden_states, w_in, w_out, ln_gain, passage_rows, old_index, queries, cand_t, teacher_t)
        new_index, loss, grad = refresh(fresh.reshape(-1, fresh.shape[-1]), places, loss, grad, old_index)
        return new_index, loss.reshape(-1), grad

    return jax.shard_map(
        local,
        mesh=mesh,
        in_specs=(
            P(("loader", "shard"), None),
            P(),
            P(),
            P(),
            P(("loader", "shard")),
            P("shard", None),
            P("loader", None),
            P("loader", None),
            P("loader", None),
        ),
        out_specs=(P("shard", None), P(("loader", "shard")), P(("loader", "shard"), None)),
        check_vma=False,
    )
```

```python
import functools

import jax
import jax.numpy as jnp
from jax import lax
from jax.experimental import pallas as pl
from jax.experimental.pallas import tpu as pltpu
from jax.sharding import PartitionSpec as P

LEN = 256
EPS = 1e-05
MIB = 2**20
MESH = pl.DeviceIdType.MESH
BF16, F32, I32 = jnp.bfloat16, jnp.float32, jnp.int32
NONE = -1e30


def gelu(v):
    return 0.5 * v * (1.0 + lax.erf(v * 0.7071067811865476))


def main_kernel(block, chunk, loaders, shards,
                x_hbm, win_hbm, wout_hbm, gain_ref, rows_ref, old_hbm, q_ref, cand_ref, teacher_ref,
                loss_ref, grad_ref, fresh_ref, place_ref,
                x, win, wout, inner, mixed, fresh, old, s_all, a_s, hi_s, lo_s, t_map, got, flat, spread, w_s,
                ids, ids_a, ids_b, slots, mine, packed, stats, tot, pair, part, own, inbox,
                load_sem, ids1_send, ids1_recv, ids2_send, ids2_recv,
                send1, recv1, send2, recv2, send3, recv3, send4, recv4, send5, recv5):
    tokens, d = x.shape
    ff = win.shape[1]
    rows = old.shape[0]
    k, nq = cand_ref.shape
    per = nq // shards
    blocks, chunks = tokens // block, ff // chunk
    his = rows // 128
    places = loaders * 2 * shards
    ext = his + places // 128
    li, si = lax.axis_index("loader"), lax.axis_index("shard")
    shard_peers = [(li, lax.rem(si + j, shards)) for j in range(1, shards)]
    loader_peers = [(lax.rem(li + j, loaders), si) for j in range(1, loaders)]

    half, head = ff // 2, pl.ds(0, block)
    rest = pl.ds(block, tokens - block)
    jobs = [pltpu.make_async_copy(src, dst, load_sem.at[i]) for i, (src, dst) in enumerate([
        (x_hbm.at[head], x.at[head]),
        (win_hbm.at[:, pl.ds(0, half)], win.at[:, pl.ds(0, half)]),
        (win_hbm.at[:, pl.ds(half, half)], win.at[:, pl.ds(half, half)]),
        (wout_hbm, wout), (x_hbm.at[rest], x.at[rest]), (old_hbm, old)])]
    for job in jobs[:5]:
        job.start()
    barrier = pltpu.get_barrier_semaphore()
    for peer in shard_peers + loader_peers:
        pl.semaphore_signal(barrier, inc=1, device_id=peer, device_id_type=MESH)

    def send(src, dst, sends, recvs, peers):
        copies = []
        for j, peer in enumerate(peers):
            copy = pltpu.make_async_remote_copy(
                src_ref=src(peer), dst_ref=dst, send_sem=sends.at[j], recv_sem=recvs.at[j],
                device_id=peer, device_id_type=MESH)
            copy.start()
            copies.append(copy)
        return copies

    def arrive(copies):
        for copy in copies:
            copy.wait_recv()

    started = []

    def norm(b):
        for j in range(block // LEN):
            y = mixed[b % 2, j * LEN:(j + 1) * LEN, :]
            centered = y - jnp.mean(y, axis=-1, keepdims=True)
            var = jnp.mean(centered * centered, axis=-1, keepdims=True)
            normed = centered * lax.rsqrt(var + EPS)
            n = b * (block // LEN) + j
            fresh[n:n + 1, :] = jnp.sum(normed, axis=0, keepdims=True) * (1.0 / LEN) * gain_ref[...].reshape(1, d)

    def encode_block(b):
        rs = slice(b * block, (b + 1) * block)
        for c in range(chunks):
            cs = slice(c * chunk, (c + 1) * chunk)
            if b == 0 and c * chunk == half:
                jobs[2].wait()
            h = jnp.dot(x[rs, :], win[:, cs], preferred_element_type=F32)
            inner[b % 2, :, cs] = gelu(h).astype(BF16)
            if c == 0 and b > 0:
                norm(b - 1)
        if b == 0:
            jobs[3].wait()
            jobs[4].wait()
        mixed[b % 2] = x[rs, :].astype(F32) + jnp.dot(inner[b % 2], wout[...], preferred_element_type=F32)

    jobs[0].wait()
    jobs[1].wait()
    encode_block(0)
    jobs[5].start()

    passages = tokens // LEN
    lane8 = lax.broadcasted_iota(I32, (8, 128), 1)
    numbers = [rows_ref[p] for p in range(passages)]
    block_ids = jnp.full((8, 128), -1, I32)
    for p in range(passages):
        block_ids = jnp.where(lane8 == p, numbers[p], block_ids)
    ids[...] = block_ids
    pl.semaphore_wait(barrier, shards + loaders - 2)
    ids_a[si] = block_ids
    sent = send(lambda peer: ids, ids_a.at[si], ids1_send, ids1_recv, shard_peers)
    started += sent
    encode_block(1)
    arrive(sent)
    seen = jnp.concatenate([ids_a[s, 0:1, :] for s in range(shards)], axis=0)
    mine_mask = (seen >= si * rows) & (seen < (si + 1) * rows)
    lane_f = lane8.astype(F32)
    value = (seen - si * rows).astype(F32)
    at0 = jnp.min(jnp.where(mine_mask, lane_f, 999.0), axis=1, keepdims=True)
    at1 = jnp.min(jnp.where(mine_mask & (lane_f != at0), lane_f, 999.0), axis=1, keepdims=True)
    for r, at in enumerate((at0, at1)):
        found = jnp.sum(jnp.where(lane_f == at, value, 0.0), axis=1, keepdims=True)
        ids_b[li, r * shards:(r + 1) * shards, :] = jnp.broadcast_to(jnp.where(at < 900.0, found, -1.0), (8, 128))
    sent = send(lambda peer: ids_b.at[li], ids_b.at[li], ids2_send, ids2_recv, loader_peers)
    started += sent
    for b in range(2, blocks):
        encode_block(b)
    norm(blocks - 1)

    owner = [i // rows for i in numbers]
    slot_iota = lax.broadcasted_iota(I32, (2 * shards, d), 0)
    filled = jnp.zeros((2 * shards, d), F32)
    for p in range(passages):
        rank = sum([(owner[o] == owner[p]).astype(I32) for o in range(p)], jnp.int32(0))
        filled = jnp.where(slot_iota == owner[p] * 2 + rank, fresh[p:p + 1, :], filled)
    for s in range(shards):
        slots[s] = filled[2 * s:2 * s + 2, :]
    mine[si] = slots[si]
    sent_a = send(lambda peer: slots.at[peer[1]], mine.at[si], send1, recv1, shard_peers)
    started += sent_a

    jobs[5].wait()
    tile = 512
    for t in range(rows // tile):
        rs = slice(t * tile, (t + 1) * tile)
        s_all[:, rs] = lax.dot_general(q_ref[...], old[rs, :], (((1,), (1,)), ((), ())), preferred_element_type=F32)

    arrive(sent_a)
    for s in range(shards):
        for r in range(2):
            packed[r * shards + s:r * shards + s + 1, :] = mine[s, r:r + 1, :]
    fresh_ref[li] = packed[...].astype(BF16)
    sent_b = send(lambda peer: fresh_ref.at[li], fresh_ref.at[li], send2, recv2, loader_peers)
    started += sent_b

    arrive(sent)
    where_to = ids_b[...].reshape(places, 128).T[0:8, :]
    place_ref[...] = where_to
    place_i = where_to[0:1, :].astype(I32)
    left = jnp.where(lax.broadcasted_iota(I32, (his, places), 0) == (place_i >> 7),
                     (lax.broadcasted_iota(I32, (his, places), 1) + 1).astype(F32), 0.0).astype(BF16)
    right = jnp.where(lax.broadcasted_iota(I32, (128, places), 0) == (place_i & 127), 1.0, 0.0).astype(BF16)
    t_map[...] = lax.dot_general(left, right, (((1,), (1,)), ((), ())), preferred_element_type=F32)

    local = cand_ref[...] - si * rows
    owned = (local >= 0) & (local < rows)
    high = jnp.where(owned, local >> 7, -1)
    low = local & 127
    hi_s[...] = jnp.concatenate([high, high], axis=0).T
    lo_s[...] = jnp.concatenate([low, low], axis=0).T

    lane = lax.broadcasted_iota(I32, (8, 2 * k), 1)
    sub = lax.broadcasted_iota(I32, (8, 2 * k), 0)
    masks = [lane // k + 2 * v == sub for v in range(4)]

    def pick(g, carry):
        qs = pl.ds(pl.multiple_of(g * 8, 8), 8)
        hi, lo = hi_s[qs, :], lo_s[qs, :]
        out = jnp.zeros((8, 128), F32)
        spot = jnp.zeros((8, 128), F32)
        for h in range(his):
            here = hi == h
            out = jnp.where(here, jnp.take_along_axis(
                s_all[qs, h * 128:(h + 1) * 128], lo, axis=1, mode="promise_in_bounds"), out)
            spot = jnp.where(here, jnp.take_along_axis(
                jnp.broadcast_to(t_map[h:h + 1, :], (8, 128)), lo, axis=1, mode="promise_in_bounds"), spot)
        is_fresh = spot > 0.5
        slot = spot.astype(I32) - 1
        hi = jnp.where(is_fresh, his + (slot >> 7), hi)
        lo = jnp.where(is_fresh, slot & 127, lo)
        hi_s[qs, :] = hi
        lo_s[qs, :] = lo
        got[qs, :] = out
        lo_f = lo.astype(F32)
        flat[g] = jnp.broadcast_to(jnp.concatenate(
            [jnp.sum(jnp.where(m, lo_f, 0.0), axis=0, keepdims=True) for m in masks], axis=1), (8, 8 * k))
        wide = jnp.concatenate([jnp.where(m, hi, -1) for m in masks], axis=1)
        a_s[g] = jnp.concatenate([jnp.where(wide == h, 1.0, 0.0) for h in range(ext)], axis=0).astype(BF16)
        return carry

    lax.fori_loop(0, nq // 8, pick, 0)
    teacher = teacher_ref[...]
    shifted = teacher - jnp.max(teacher, axis=0, keepdims=True)
    log_t = shifted - jnp.log(jnp.sum(jnp.exp(shifted), axis=0, keepdims=True))
    p_t = jnp.exp(log_t)
    entropy = jnp.sum(p_t * log_t, axis=0, keepdims=True)

    arrive(sent_b)
    rows_f = fresh_ref[...].reshape(places, d)
    s_fresh = lax.dot_general(q_ref[...], rows_f, (((1,), (1,)), ((), ())), preferred_element_type=F32)
    s_all[:, 0:places] = s_fresh

    def pick_fresh(g, carry):
        qs = pl.ds(pl.multiple_of(g * 8, 8), 8)
        hi, lo = hi_s[qs, :], lo_s[qs, :]
        out = got[qs, :]
        for h in range(places // 128):
            out = jnp.where(hi == his + h, jnp.take_along_axis(
                s_all[qs, h * 128:(h + 1) * 128], lo, axis=1, mode="promise_in_bounds"), out)
        got[qs, :] = out
        return carry

    lax.fori_loop(0, nq // 8, pick_fresh, 0, unroll=8)
    score = got[...].T[0:k, :]
    top = jnp.max(jnp.where(owned, score, NONE), axis=0, keepdims=True)
    diff = score - top
    z = jnp.sum(jnp.where(owned, jnp.exp(jnp.where(owned, diff, 0.0)), 0.0), axis=0, keepdims=True)
    a = jnp.sum(jnp.where(owned, p_t * diff, 0.0), axis=0, keepdims=True)
    b = jnp.sum(jnp.where(owned, p_t, 0.0), axis=0, keepdims=True)
    stats[si] = jnp.concatenate([top, z, a, b, top, z, a, b], axis=0)
    sent_s = send(lambda peer: stats.at[si], stats.at[si], send3, recv3, shard_peers)
    started += sent_s
    arrive(sent_s)
    every = [stats[s] for s in range(shards)]
    top = functools.reduce(jnp.maximum, [e[0:1] for e in every])
    z = sum([e[1:2] * jnp.exp(e[0:1] - top) for e in every])
    cross = sum([e[2:3] + e[3:4] * (e[0:1] - top) for e in every])
    log_z = jnp.log(z)
    loss = entropy - cross + log_z
    out = jnp.zeros((1, per), F32)
    for s in range(shards):
        out = jnp.where(si == s, loss[:, s * per:(s + 1) * per], out)
    loss_ref[...] = out
    student = jnp.exp(jnp.where(owned, score - top - log_z, 0.0))
    weight = jnp.where(owned, student - p_t, 0.0).astype(BF16).astype(F32)
    w_s[...] = jnp.concatenate([weight, weight], axis=0).T

    lo_iota = lax.broadcasted_iota(I32, (128, 8 * k), 0).astype(F32)

    def group(g):
        w2 = w_s[pl.ds(pl.multiple_of(g * 8, 8), 8), :]
        w_flat = jnp.concatenate(
            [jnp.sum(jnp.where(m, w2, 0.0), axis=0, keepdims=True) for m in masks], axis=1)
        right = jnp.where(lo_iota == flat[g][0:1, :], w_flat, 0.0).astype(BF16)
        return lax.dot_general(a_s[g], right, (((1,), (1,)), ((), ())), preferred_element_type=F32)

    def place(g, carry):
        one, two = group(g * 2), group(g * 2 + 1)
        qs = pl.ds(pl.multiple_of(g * 16, 16), 16)
        for h in range(ext):
            both = jnp.concatenate([one[h * 8:(h + 1) * 8], two[h * 8:(h + 1) * 8]], axis=0)
            spread[qs, h * 128:(h + 1) * 128] = both.astype(BF16)
        return carry

    lax.fori_loop(0, nq // 16, place, 0, unroll=4)
    core, y = lax.rem(si, 2), si // 2
    ys = shards // 2
    mate = (li, 2 * y + 1 - core)
    wide = d // 2

    def partial(c):
        cs = slice(c * wide, (c + 1) * wide)
        total = (jnp.dot(spread[:, 0:rows], old[:, cs], preferred_element_type=F32)
                 + jnp.dot(spread[:, rows:rows + places], fresh_ref[...].reshape(places, d)[:, cs],
                           preferred_element_type=F32))
        for s in range(shards):
            tot[c, s % 2, s // 2] = total[s * per:(s + 1) * per, :]
        copy = pltpu.make_async_remote_copy(
            src_ref=tot.at[c, 1 - core], dst_ref=pair.at[c], send_sem=send5.at[c], recv_sem=recv5.at[c],
            device_id=mate, device_id_type=MESH)
        copy.start()
        return copy

    def pass_on(c, copy):
        copy.wait_recv()
        for t in range(ys):
            part[c, t] = (tot[c, core, t] + pair[c, t]).astype(BF16)
        copies = []
        for j in range(1, ys):
            to = lax.rem(y + j, ys)
            copy = pltpu.make_async_remote_copy(
                src_ref=part.at[c, to], dst_ref=inbox.at[c, j - 1], send_sem=send4.at[c, j - 1],
                recv_sem=recv4.at[c, j - 1], device_id=(li, 2 * to + core), device_id_type=MESH)
            copy.start()
            copies.append(copy)
        own[c] = tot[c, core, y] + pair[c, y]
        return copies

    first = partial(0)
    second = partial(1)
    sent_0 = pass_on(0, first)
    sent_1 = pass_on(1, second)
    for c, copies in enumerate((sent_0, sent_1)):
        acc = own[c]
        for j, copy in enumerate(copies):
            copy.wait_recv()
            acc = acc + inbox[c, j].astype(F32)
        grad_ref[:, c * wide:(c + 1) * wide] = acc
    sent_g = [first, second] + sent_0 + sent_1
    for copy in started + sent_g:
        copy.wait_send()


def main(loaders, shards, hidden, w_in, w_out, gain, passage_rows, old_index, queries, cand_t, teacher_t):
    tokens, d = hidden.shape
    ff = w_in.shape[1]
    rows = old_index.shape[0]
    k, nq = cand_t.shape
    per = nq // shards
    places = loaders * 2 * shards
    ext = (rows + places) // 128
    block, chunk = 512, 768
    anywhere = pl.BlockSpec(memory_space=pl.ANY)
    vmem = pl.BlockSpec(memory_space=pltpu.VMEM)
    smem = pl.BlockSpec(memory_space=pltpu.SMEM)
    dma = pltpu.SemaphoreType.DMA
    return pl.pallas_call(
        functools.partial(main_kernel, block, chunk, loaders, shards),
        out_shape=[
            jax.ShapeDtypeStruct((1, per), F32),
            jax.ShapeDtypeStruct((per, d), F32),
            jax.ShapeDtypeStruct((loaders, 2 * shards, d), BF16),
            jax.ShapeDtypeStruct((8, places), F32),
        ],
        in_specs=[anywhere] * 3 + [vmem, smem, anywhere, vmem, vmem, vmem],
        out_specs=[vmem] * 4,
        scratch_shapes=[
            pltpu.VMEM((tokens, d), BF16),
            pltpu.VMEM((d, ff), BF16),
            pltpu.VMEM((ff, d), BF16),
            pltpu.VMEM((2, block, ff), BF16),
            pltpu.VMEM((2, block, d), F32),
            pltpu.VMEM((tokens // LEN, d), F32),
            pltpu.VMEM((rows, d), BF16),
            pltpu.VMEM((nq, rows), F32),
            pltpu.VMEM((nq // 8, 8 * ext, 8 * k), BF16),
            pltpu.VMEM((nq, 2 * k), I32),
            pltpu.VMEM((nq, 2 * k), I32),
            pltpu.VMEM((rows // 128, 128), F32),
            pltpu.VMEM((nq, 2 * k), F32),
            pltpu.VMEM((nq // 8, 8, 8 * k), F32),
            pltpu.VMEM((nq, 128 * ext), BF16),
            pltpu.VMEM((nq, 2 * k), F32),
            pltpu.VMEM((8, 128), I32),
            pltpu.VMEM((shards, 8, 128), I32),
            pltpu.VMEM((loaders, 2 * shards, 128), F32),
            pltpu.VMEM((shards, 2, d), F32),
            pltpu.VMEM((shards, 2, d), F32),
            pltpu.VMEM((2 * shards, d), F32),
            pltpu.VMEM((shards, 8, nq), F32),
            pltpu.VMEM((2, 2, shards // 2, per, d // 2), F32),
            pltpu.VMEM((2, shards // 2, per, d // 2), F32),
            pltpu.VMEM((2, shards // 2, per, d // 2), BF16),
            pltpu.VMEM((2, per, d // 2), F32),
            pltpu.VMEM((2, shards // 2, per, d // 2), BF16),
            dma((6,)),
            dma((shards,)), dma((shards,)), dma((loaders,)), dma((loaders,)),
            dma((shards,)), dma((shards,)), dma((loaders,)), dma((loaders,)),
            dma((shards,)), dma((shards,)), dma((2, shards)), dma((2, shards)), dma((2,)), dma((2,)),
        ],
        compiler_params=pltpu.CompilerParams(collective_id=0, has_side_effects=True, vmem_limit_bytes=60 * MIB),
        name="main",
    )(hidden, w_in, w_out, gain, passage_rows, old_index, queries, cand_t, teacher_t)


def index_kernel(tile, fresh_hbm, place_hbm, loss_hbm, grad_hbm, old_hbm, new_hbm, loss_out, grad_out,
                 fresh_ref, place_ref, old, new, side_sem, in_sem, out_sem):
    rows, d = old.shape
    tiles = rows // tile
    sides = [pltpu.make_async_copy(src, dst, side_sem.at[i]) for i, (src, dst) in enumerate(
        [(place_hbm, place_ref), (fresh_hbm, fresh_ref), (loss_hbm, loss_out), (grad_hbm, grad_out)])]
    loads = [pltpu.make_async_copy(old_hbm.at[pl.ds(t * tile, tile)], old.at[pl.ds(t * tile, tile)], in_sem.at[t])
             for t in range(tiles)]
    for load in sides[0:2] + loads + sides[2:4]:
        load.start()
    sides[0].wait()
    sides[1].wait()
    where_to = place_ref[0:1, :].astype(I32)
    places = fresh_ref.shape[0]
    ones = jnp.ones((places, 128), BF16)
    row_iota = lax.broadcasted_iota(I32, (tile, places), 0)
    stores = []
    for t in range(tiles):
        rs = slice(t * tile, (t + 1) * tile)
        place = jnp.where(row_iota + t * tile == where_to, 1.0, 0.0).astype(BF16)
        put = jnp.dot(place, fresh_ref[...], preferred_element_type=F32)
        has = jnp.dot(place, ones, preferred_element_type=F32)
        loads[t].wait()
        for c in range(d // 128):
            cs = slice(c * 128, (c + 1) * 128)
            new[rs, cs] = jnp.where(has > 0.5, put[:, cs], old[rs, cs].astype(F32)).astype(BF16)
        store = pltpu.make_async_copy(new.at[pl.ds(t * tile, tile)], new_hbm.at[pl.ds(t * tile, tile)], out_sem.at[t])
        store.start()
        stores.append(store)
    for store in stores + sides[2:4]:
        store.wait()


def refresh(fresh, places, loss, grad, old_index):
    rows, d = old_index.shape
    tile = 512
    anywhere = pl.BlockSpec(memory_space=pl.ANY)
    return pl.pallas_call(
        functools.partial(index_kernel, tile),
        out_shape=[jax.ShapeDtypeStruct((rows, d), BF16), jax.ShapeDtypeStruct(loss.shape, F32),
                   jax.ShapeDtypeStruct(grad.shape, F32)],
        in_specs=[anywhere] * 5,
        out_specs=[anywhere] * 3,
        scratch_shapes=[
            pltpu.VMEM(fresh.shape, BF16),
            pltpu.VMEM(places.shape, F32),
            pltpu.VMEM((rows, d), BF16),
            pltpu.VMEM((rows, d), BF16),
            pltpu.SemaphoreType.DMA((4,)),
            pltpu.SemaphoreType.DMA((rows // tile,)),
            pltpu.SemaphoreType.DMA((rows // tile,)),
        ],
        compiler_params=pltpu.CompilerParams(vmem_limit_bytes=60 * MIB),
        name="refresh",
    )(fresh, places, loss, grad, old_index)


def solution(mesh):
    loaders, shards = mesh.shape["loader"], mesh.shape["shard"]

    def local(hidden_states, w_in, w_out, ln_gain, passage_rows, old_index, queries, candidates, teacher):
        cand_t, teacher_t = candidates.T, teacher.T
        loss, grad, fresh, places = main(
            loaders, shards, hidden_states, w_in, w_out, ln_gain, passage_rows, old_index, queries, cand_t, teacher_t)
        new_index, loss, grad = refresh(fresh.reshape(-1, fresh.shape[-1]), places, loss, grad, old_index)
        return new_index, loss.reshape(-1), grad

    return jax.shard_map(
        local,
        mesh=mesh,
        in_specs=(
            P(("loader", "shard"), None),
            P(),
            P(),
            P(),
            P(("loader", "shard")),
            P("shard", None),
            P("loader", None),
            P("loader", None),
            P("loader", None),
        ),
        out_specs=(P("shard", None), P(("loader", "shard")), P(("loader", "shard"), None)),
        check_vma=False,
    )
```

```python
import functools

import jax
import jax.numpy as jnp
from jax import lax
from jax.experimental import pallas as pl
from jax.experimental.pallas import tpu as pltpu
from jax.sharding import PartitionSpec as P

LEN = 256
EPS = 1e-05
MIB = 2**20
MESH = pl.DeviceIdType.MESH
BF16, F32, I32 = jnp.bfloat16, jnp.float32, jnp.int32
NONE = -1e30


def gelu(v):
    return 0.5 * v * (1.0 + lax.erf(v * 0.7071067811865476))


def main_kernel(block, chunk, loaders, shards,
                x_hbm, win_hbm, wout_hbm, gain_ref, rows_ref, old_hbm, q_ref, cand_ref, teacher_ref,
                loss_ref, grad_ref, old,
                x, win, wout, inner, mixed, fresh, fresh_ref, s_all, a_s, hi_s, lo_s, t_map, got, r_s, spread, w_s,
                ids, ids_a, ids_b, slots, mine, packed, stats, tot, pair, part, own, inbox,
                load_sem, ids1_send, ids1_recv, ids2_send, ids2_recv,
                send1, recv1, send2, recv2, send3, recv3, send4, recv4, send5, recv5):
    tokens, d = x.shape
    ff = win.shape[1]
    rows = old.shape[0]
    k, nq = cand_ref.shape
    per = nq // shards
    blocks, chunks = tokens // block, ff // chunk
    his = rows // 128
    places = loaders * 2 * shards
    ext = (rows + places) // 256
    pads = ext + ext % 2
    li, si = lax.axis_index("loader"), lax.axis_index("shard")
    shard_peers = [(li, lax.rem(si + j, shards)) for j in range(1, shards)]
    loader_peers = [(lax.rem(li + j, loaders), si) for j in range(1, loaders)]

    half, head = ff // 2, pl.ds(0, block)
    rest = pl.ds(block, tokens - block)
    jobs = [pltpu.make_async_copy(src, dst, load_sem.at[i]) for i, (src, dst) in enumerate([
        (x_hbm.at[head], x.at[head]),
        (win_hbm.at[:, pl.ds(0, half)], win.at[:, pl.ds(0, half)]),
        (win_hbm.at[:, pl.ds(half, half)], win.at[:, pl.ds(half, half)]),
        (wout_hbm, wout), (x_hbm.at[rest], x.at[rest]), (old_hbm, old)])]
    for job in jobs[:5]:
        job.start()
    barrier = pltpu.get_barrier_semaphore()
    for peer in shard_peers + loader_peers:
        pl.semaphore_signal(barrier, inc=1, device_id=peer, device_id_type=MESH)

    def send(src, dst, sends, recvs, peers):
        copies = []
        for j, peer in enumerate(peers):
            copy = pltpu.make_async_remote_copy(
                src_ref=src(peer), dst_ref=dst, send_sem=sends.at[j], recv_sem=recvs.at[j],
                device_id=peer, device_id_type=MESH)
            copy.start()
            copies.append(copy)
        return copies

    def arrive(copies):
        for copy in copies:
            copy.wait_recv()

    started = []

    def norm(b):
        for j in range(block // LEN):
            y = mixed[b % 2, j * LEN:(j + 1) * LEN, :]
            centered = y - jnp.mean(y, axis=-1, keepdims=True)
            var = jnp.mean(centered * centered, axis=-1, keepdims=True)
            normed = centered * lax.rsqrt(var + EPS)
            n = b * (block // LEN) + j
            fresh[n:n + 1, :] = jnp.sum(normed, axis=0, keepdims=True) * (1.0 / LEN) * gain_ref[...].reshape(1, d)

    def encode_block(b):
        rs = slice(b * block, (b + 1) * block)
        for c in range(chunks):
            cs = slice(c * chunk, (c + 1) * chunk)
            if b == 0 and c * chunk == half:
                jobs[2].wait()
            h = jnp.dot(x[rs, :], win[:, cs], preferred_element_type=F32)
            inner[b % 2, :, cs] = gelu(h).astype(BF16)
            if c == 0 and b > 0:
                norm(b - 1)
        if b == 0:
            jobs[3].wait()
            jobs[4].wait()
        mixed[b % 2] = x[rs, :].astype(F32) + jnp.dot(inner[b % 2], wout[...], preferred_element_type=F32)

    jobs[0].wait()
    jobs[1].wait()
    encode_block(0)
    jobs[5].start()

    passages = tokens // LEN
    lane8 = lax.broadcasted_iota(I32, (8, 128), 1)
    numbers = [rows_ref[p] for p in range(passages)]
    block_ids = jnp.full((8, 128), -1, I32)
    for p in range(passages):
        block_ids = jnp.where(lane8 == p, numbers[p], block_ids)
    ids[...] = block_ids
    pl.semaphore_wait(barrier, shards + loaders - 2)
    ids_a[si] = block_ids
    sent = send(lambda peer: ids, ids_a.at[si], ids1_send, ids1_recv, shard_peers)
    started += sent
    encode_block(1)
    arrive(sent)
    seen = jnp.concatenate([ids_a[s, 0:1, :] for s in range(shards)], axis=0)
    mine_mask = (seen >= si * rows) & (seen < (si + 1) * rows)
    lane_f = lane8.astype(F32)
    value = (seen - si * rows).astype(F32)
    at0 = jnp.min(jnp.where(mine_mask, lane_f, 999.0), axis=1, keepdims=True)
    at1 = jnp.min(jnp.where(mine_mask & (lane_f != at0), lane_f, 999.0), axis=1, keepdims=True)
    for r, at in enumerate((at0, at1)):
        found = jnp.sum(jnp.where(lane_f == at, value, 0.0), axis=1, keepdims=True)
        ids_b[li, r * shards:(r + 1) * shards, :] = jnp.broadcast_to(jnp.where(at < 900.0, found, -1.0), (8, 128))
    sent = send(lambda peer: ids_b.at[li], ids_b.at[li], ids2_send, ids2_recv, loader_peers)
    started += sent
    for b in range(2, blocks):
        encode_block(b)
    norm(blocks - 1)

    owner = [i // rows for i in numbers]
    slot_iota = lax.broadcasted_iota(I32, (2 * shards, d), 0)
    filled = jnp.zeros((2 * shards, d), F32)
    for p in range(passages):
        rank = sum([(owner[o] == owner[p]).astype(I32) for o in range(p)], jnp.int32(0))
        filled = jnp.where(slot_iota == owner[p] * 2 + rank, fresh[p:p + 1, :], filled)
    for s in range(shards):
        slots[s] = filled[2 * s:2 * s + 2, :]
    mine[si] = slots[si]
    sent_a = send(lambda peer: slots.at[peer[1]], mine.at[si], send1, recv1, shard_peers)
    started += sent_a

    jobs[5].wait()
    tile = 512
    for t in range(rows // tile):
        rs = slice(t * tile, (t + 1) * tile)
        s_all[:, rs] = lax.dot_general(q_ref[...], old[rs, :], (((1,), (1,)), ((), ())), preferred_element_type=F32)

    arrive(sent_a)
    for s in range(shards):
        for r in range(2):
            packed[r * shards + s:r * shards + s + 1, :] = mine[s, r:r + 1, :]
    fresh_ref[li] = packed[...].astype(BF16)
    sent_b = send(lambda peer: fresh_ref.at[li], fresh_ref.at[li], send2, recv2, loader_peers)
    started += sent_b

    arrive(sent)
    where_to = ids_b[...].reshape(places, 128).T[0:8, :]
    place_i = where_to[0:1, :].astype(I32)
    left = jnp.where(lax.broadcasted_iota(I32, (his, places), 0) == (place_i >> 7),
                     (lax.broadcasted_iota(I32, (his, places), 1) + 1).astype(F32), 0.0).astype(BF16)
    right = jnp.where(lax.broadcasted_iota(I32, (128, places), 0) == (place_i & 127), 1.0, 0.0).astype(BF16)
    t_map[...] = lax.dot_general(left, right, (((1,), (1,)), ((), ())), preferred_element_type=F32)

    local = cand_ref[...] - si * rows
    owned = (local >= 0) & (local < rows)
    high = jnp.where(owned, local >> 7, -1)
    low = local & 127
    hi_s[...] = jnp.concatenate([high, high], axis=0).T
    lo_s[...] = jnp.concatenate([low, low], axis=0).T

    lane = lax.broadcasted_iota(I32, (8, 2 * k), 1)
    sub = lax.broadcasted_iota(I32, (8, 2 * k), 0)
    masks = [lane // k + 2 * v == sub for v in range(4)]

    lo_iota = lax.broadcasted_iota(I32, (256, 8 * k), 0).astype(F32)

    def pick(g, carry):
        qs = pl.ds(pl.multiple_of(g * 8, 8), 8)
        hi, lo = hi_s[qs, :], lo_s[qs, :]
        out = jnp.zeros((8, 128), F32)
        spot = jnp.zeros((8, 128), F32)
        for h in range(his):
            here = hi == h
            out = jnp.where(here, jnp.take_along_axis(
                s_all[qs, h * 128:(h + 1) * 128], lo, axis=1, mode="promise_in_bounds"), out)
            spot = jnp.where(here, jnp.take_along_axis(
                jnp.broadcast_to(t_map[h:h + 1, :], (8, 128)), lo, axis=1, mode="promise_in_bounds"), spot)
        is_fresh = spot > 0.5
        slot = spot.astype(I32) - 1
        hi = jnp.where(is_fresh, his + (slot >> 7), hi)
        lo = jnp.where(is_fresh, slot & 127, lo)
        hi_s[qs, :] = hi
        lo_s[qs, :] = lo
        got[qs, :] = out
        lo_f = (lo + (hi & 1) * 128).astype(F32)
        low_flat = jnp.concatenate(
            [jnp.sum(jnp.where(m, lo_f, 0.0), axis=0, keepdims=True) for m in masks], axis=1)
        r_s[g] = jnp.where(lo_iota == low_flat, 1.0, 0.0).astype(BF16)
        wide = jnp.concatenate([jnp.where(m, hi >> 1, -1) for m in masks], axis=1)
        a_s[g] = jnp.concatenate([jnp.where(wide == h, 1.0, 0.0) for h in range(pads)], axis=0).astype(BF16)
        return carry

    lax.fori_loop(0, nq // 8, pick, 0)
    teacher = teacher_ref[...]
    shifted = teacher - jnp.max(teacher, axis=0, keepdims=True)
    log_t = shifted - jnp.log(jnp.sum(jnp.exp(shifted), axis=0, keepdims=True))
    p_t = jnp.exp(log_t)
    entropy = jnp.sum(p_t * log_t, axis=0, keepdims=True)

    arrive(sent_b)
    rows_f = fresh_ref[...].reshape(places, d)
    s_fresh = lax.dot_general(q_ref[...], rows_f, (((1,), (1,)), ((), ())), preferred_element_type=F32)
    s_all[:, 0:places] = s_fresh

    def pick_fresh(g, carry):
        qs = pl.ds(pl.multiple_of(g * 8, 8), 8)
        hi, lo = hi_s[qs, :], lo_s[qs, :]
        out = got[qs, :]
        for h in range(places // 128):
            out = jnp.where(hi == his + h, jnp.take_along_axis(
                s_all[qs, h * 128:(h + 1) * 128], lo, axis=1, mode="promise_in_bounds"), out)
        got[qs, :] = out
        return carry

    lax.fori_loop(0, nq // 8, pick_fresh, 0, unroll=16)
    score = got[...].T[0:k, :]
    top = jnp.max(jnp.where(owned, score, NONE), axis=0, keepdims=True)
    diff = score - top
    z = jnp.sum(jnp.where(owned, jnp.exp(jnp.where(owned, diff, 0.0)), 0.0), axis=0, keepdims=True)
    a = jnp.sum(jnp.where(owned, p_t * diff, 0.0), axis=0, keepdims=True)
    b = jnp.sum(jnp.where(owned, p_t, 0.0), axis=0, keepdims=True)
    stats[si] = jnp.concatenate([top, z, a, b, top, z, a, b], axis=0)
    sent_s = send(lambda peer: stats.at[si], stats.at[si], send3, recv3, shard_peers)
    started += sent_s
    arrive(sent_s)
    every = [stats[s] for s in range(shards)]
    top = functools.reduce(jnp.maximum, [e[0:1] for e in every])
    z = sum([e[1:2] * jnp.exp(e[0:1] - top) for e in every])
    cross = sum([e[2:3] + e[3:4] * (e[0:1] - top) for e in every])
    log_z = jnp.log(z)
    loss = entropy - cross + log_z
    out = jnp.zeros((1, per), F32)
    for s in range(shards):
        out = jnp.where(si == s, loss[:, s * per:(s + 1) * per], out)
    loss_ref[...] = out
    student = jnp.exp(jnp.where(owned, score - top - log_z, 0.0))
    weight = jnp.where(owned, student - p_t, 0.0).astype(BF16).astype(F32)
    w_s[...] = jnp.concatenate([weight, weight], axis=0).T

    def group(g):
        w2 = w_s[pl.ds(pl.multiple_of(g * 8, 8), 8), :]
        w_flat = jnp.concatenate(
            [jnp.sum(jnp.where(m, w2, 0.0), axis=0, keepdims=True) for m in masks], axis=1)
        w_16 = jnp.broadcast_to(w_flat, (16, 8 * k)).astype(BF16)
        left = (a_s[g].reshape(pads // 2, 16, 8 * k) * w_16[None]).reshape(8 * pads, 8 * k)
        return lax.dot_general(left, r_s[g], (((1,), (1,)), ((), ())), preferred_element_type=F32)

    def place(g, carry):
        one, two = group(g * 2), group(g * 2 + 1)
        qs = pl.ds(pl.multiple_of(g * 16, 16), 16)
        for h in range(ext):
            both = jnp.concatenate([one[h * 8:(h + 1) * 8], two[h * 8:(h + 1) * 8]], axis=0)
            spread[qs, h * 256:(h + 1) * 256] = both.astype(BF16)
        return carry

    lax.fori_loop(0, nq // 16, place, 0, unroll=4)
    core, y = lax.rem(si, 2), si // 2
    ys = shards // 2
    mate = (li, 2 * y + 1 - core)
    wide = d // 2

    def partial(c):
        cs = slice(c * wide, (c + 1) * wide)
        total = (jnp.dot(spread[:, 0:rows], old[:, cs], preferred_element_type=F32)
                 + jnp.dot(spread[:, rows:rows + places], fresh_ref[...].reshape(places, d)[:, cs],
                           preferred_element_type=F32))
        for s in range(shards):
            tot[c, s % 2, s // 2] = total[s * per:(s + 1) * per, :]
        copy = pltpu.make_async_remote_copy(
            src_ref=tot.at[c, 1 - core], dst_ref=pair.at[c], send_sem=send5.at[c], recv_sem=recv5.at[c],
            device_id=mate, device_id_type=MESH)
        copy.start()
        return copy

    def pass_on(c, copy):
        copy.wait_recv()
        for t in range(ys):
            part[c, t] = (tot[c, core, t] + pair[c, t]).astype(BF16)
        copies = []
        for j in range(1, ys):
            to = lax.rem(y + j, ys)
            copy = pltpu.make_async_remote_copy(
                src_ref=part.at[c, to], dst_ref=inbox.at[c, j - 1], send_sem=send4.at[c, j - 1],
                recv_sem=recv4.at[c, j - 1], device_id=(li, 2 * to + core), device_id_type=MESH)
            copy.start()
            copies.append(copy)
        own[c] = tot[c, core, y] + pair[c, y]
        return copies

    first = partial(0)
    second = partial(1)
    sent_0 = pass_on(0, first)
    sent_1 = pass_on(1, second)

    ones = jnp.ones((places, 128), BF16)
    row_iota = lax.broadcasted_iota(I32, (tile, places), 0)
    for t in range(rows // tile):
        rs = slice(t * tile, (t + 1) * tile)
        spots = jnp.where(row_iota + t * tile == place_i, 1.0, 0.0).astype(BF16)
        put = jnp.dot(spots, fresh_ref[...].reshape(places, d), preferred_element_type=F32).astype(BF16)
        keep = (1.0 - jnp.dot(spots, ones, preferred_element_type=F32)).astype(BF16)
        for c in range(d // 128):
            cs = slice(c * 128, (c + 1) * 128)
            old[rs, cs] = old[rs, cs] * keep + put[:, cs]
    for c, copies in enumerate((sent_0, sent_1)):
        acc = own[c]
        for j, copy in enumerate(copies):
            copy.wait_recv()
            acc = acc + inbox[c, j].astype(F32)
        grad_ref[:, c * wide:(c + 1) * wide] = acc
    sent_g = [first, second] + sent_0 + sent_1
    for copy in started + sent_g:
        copy.wait_send()


def main(loaders, shards, hidden, w_in, w_out, gain, passage_rows, old_index, queries, cand_t, teacher_t):
    tokens, d = hidden.shape
    ff = w_in.shape[1]
    rows = old_index.shape[0]
    k, nq = cand_t.shape
    per = nq // shards
    places = loaders * 2 * shards
    ext = (rows + places) // 256
    block, chunk = 512, 768
    anywhere = pl.BlockSpec(memory_space=pl.ANY)
    vmem = pl.BlockSpec(memory_space=pltpu.VMEM)
    smem = pl.BlockSpec(memory_space=pltpu.SMEM)
    dma = pltpu.SemaphoreType.DMA
    return pl.pallas_call(
        functools.partial(main_kernel, block, chunk, loaders, shards),
        out_shape=[
            pltpu.VMEM((1, per), F32),
            pltpu.VMEM((per, d), F32),
            pltpu.VMEM((rows, d), BF16),
        ],
        in_specs=[anywhere] * 3 + [vmem, smem, anywhere, vmem, vmem, vmem],
        out_specs=[vmem] * 3,
        scratch_shapes=[
            pltpu.VMEM((tokens, d), BF16),
            pltpu.VMEM((d, ff), BF16),
            pltpu.VMEM((ff, d), BF16),
            pltpu.VMEM((2, block, ff), BF16),
            pltpu.VMEM((2, block, d), F32),
            pltpu.VMEM((tokens // LEN, d), F32),
            pltpu.VMEM((loaders, 2 * shards, d), BF16),
            pltpu.VMEM((nq, rows), F32),
            pltpu.VMEM((nq // 8, 8 * (ext + ext % 2), 8 * k), BF16),
            pltpu.VMEM((nq, 2 * k), I32),
            pltpu.VMEM((nq, 2 * k), I32),
            pltpu.VMEM((rows // 128, 128), F32),
            pltpu.VMEM((nq, 2 * k), F32),
            pltpu.VMEM((nq // 8, 256, 8 * k), BF16),
            pltpu.VMEM((nq, 256 * ext), BF16),
            pltpu.VMEM((nq, 2 * k), F32),
            pltpu.VMEM((8, 128), I32),
            pltpu.VMEM((shards, 8, 128), I32),
            pltpu.VMEM((loaders, 2 * shards, 128), F32),
            pltpu.VMEM((shards, 2, d), F32),
            pltpu.VMEM((shards, 2, d), F32),
            pltpu.VMEM((2 * shards, d), F32),
            pltpu.VMEM((shards, 8, nq), F32),
            pltpu.VMEM((2, 2, shards // 2, per, d // 2), F32),
            pltpu.VMEM((2, shards // 2, per, d // 2), F32),
            pltpu.VMEM((2, shards // 2, per, d // 2), BF16),
            pltpu.VMEM((2, per, d // 2), F32),
            pltpu.VMEM((2, shards // 2, per, d // 2), BF16),
            dma((6,)),
            dma((shards,)), dma((shards,)), dma((loaders,)), dma((loaders,)),
            dma((shards,)), dma((shards,)), dma((loaders,)), dma((loaders,)),
            dma((shards,)), dma((shards,)), dma((2, shards)), dma((2, shards)), dma((2,)), dma((2,)),
        ],
        compiler_params=pltpu.CompilerParams(collective_id=0, has_side_effects=True, vmem_limit_bytes=52 * MIB),
        name="main",
    )(hidden, w_in, w_out, gain, passage_rows, old_index, queries, cand_t, teacher_t)


def results_kernel(new_in, loss_in, grad_in, new_out, loss_out, grad_out, sem):
    copies = [pltpu.make_async_copy(src, dst, sem.at[i]) for i, (src, dst) in enumerate(
        [(new_in, new_out), (loss_in, loss_out), (grad_in, grad_out)])]
    for copy in copies:
        copy.start()
    for copy in copies:
        copy.wait()


def results(new, loss, grad):
    anywhere = pl.BlockSpec(memory_space=pl.ANY)
    new, loss, grad = [pltpu.with_memory_space_constraint(v, pltpu.VMEM) for v in (new, loss, grad)]
    return pl.pallas_call(
        results_kernel,
        out_shape=[jax.ShapeDtypeStruct(v.shape, v.dtype) for v in (new, loss, grad)],
        in_specs=[pl.BlockSpec(memory_space=pltpu.VMEM)] * 3,
        out_specs=[anywhere] * 3,
        scratch_shapes=[pltpu.SemaphoreType.DMA((3,))],
        compiler_params=pltpu.CompilerParams(vmem_limit_bytes=16 * MIB),
        name="results",
    )(new, loss, grad)


def solution(mesh):
    loaders, shards = mesh.shape["loader"], mesh.shape["shard"]

    def local(hidden_states, w_in, w_out, ln_gain, passage_rows, old_index, queries, candidates, teacher):
        cand_t, teacher_t = candidates.T, teacher.T
        loss, grad, new = main(
            loaders, shards, hidden_states, w_in, w_out, ln_gain, passage_rows, old_index, queries, cand_t, teacher_t)
        new_index, loss, grad = results(new, loss, grad)
        return new_index, loss.reshape(-1), grad

    return jax.shard_map(
        local,
        mesh=mesh,
        in_specs=(
            P(("loader", "shard"), None),
            P(),
            P(),
            P(),
            P(("loader", "shard")),
            P("shard", None),
            P("loader", None),
            P("loader", None),
            P("loader", None),
        ),
        out_specs=(P("shard", None), P(("loader", "shard")), P(("loader", "shard"), None)),
        check_vma=False,
    )
```
